256 devices in a mesh: rows: 256 (over z, y, x, core).
Axes of the slice: x: 4, y: 4, z: 8, core: 2. Of those that a mesh axis runs over, the one named last changes fastest.
Arguments:
- genotypes: bfloat16 [131072, 8192], P('rows'), may hold values from -40 to 40
- probes: bfloat16 [8192, 64], replicated, may hold values from -0.00018310547 to 0.00018310547
Outputs:
- projected: float32 [8192, 64], P('rows')
- r_factor: float32 [64, 64], replicated
The draws below stay inside these ranges and needn't reach their ends.
All inputs are finite; a program needn't handle non-finite values.
Results may differ from the reference program's by a relative error of at most 0.00045.
Values sent between devices are 32-bit elements; how exact they have to be, the bound alone decides.
A program may use at most 64 MiB of HBM per device.

```python
import math
import jax
import jax.numpy as jnp
from jax import lax

MARKERS = 8192
PROBES = 64
SAMPLES = 131072


def draw_genotypes(key, part):
    key = jax.random.fold_in(key, 11)
    key_noise, key_rows, key_cols = jax.random.split(key, 3)
    position = jnp.arange(SAMPLES, dtype=jnp.float32) / SAMPLES
    row_scale = (1.0 + 2.0 * position) / 3.0 * jnp.exp(jax.random.uniform(key_rows, (SAMPLES,), jnp.float32, math.log(0.3), math.log(3.0)))
    col_scale = jnp.exp(jax.random.uniform(key_cols, (MARKERS,), jnp.float32, math.log(0.3), math.log(3.0)))
    noise = jax.random.truncated_normal(key_noise, -4.0, 4.0, (SAMPLES, MARKERS), jnp.float32)
    values = noise * row_scale[:, None] * col_scale[None, :]
    return values.astype(jnp.bfloat16)


def centred(key, shape, deviation, bound, kind=jnp.bfloat16):
    result = deviation * jax.random.normal(key, shape, jnp.float32)
    return jnp.clip(result, min=-bound, max=bound).astype(kind)


def setup_inputs(seed: int = 0) -> dict:
    key_list = jax.random.split(jax.random.key(seed), 3)
    return {
        "genotypes": draw_genotypes(jax.random.fold_in(key_list[2], 71), 0),
        "probes": centred(key_list[1], (MARKERS, PROBES), (MARKERS * SAMPLES) ** -0.5, 0.00018310547),
    }


def reference(genotypes, probes):
    sketch = jnp.dot(genotypes.astype(jnp.float32), probes.astype(jnp.float32), preferred_element_type=jnp.float32)
    ortho_basis, r_factor = jnp.linalg.qr(sketch)
    sign_flip = jnp.sign(jnp.diagonal(r_factor))
    ortho_basis = ortho_basis * sign_flip[None, :]
    r_factor = r_factor * sign_flip[:, None]
    block_cols = min(MARKERS, 512)

    def project(block_index):
        column_block = lax.dynamic_slice_in_dim(genotypes, block_index * block_cols, block_cols, 1).astype(jnp.float32)
        return jnp.dot(column_block.T, ortho_basis, precision=lax.Precision.HIGHEST)
    blocks = lax.map(project, jnp.arange(MARKERS // block_cols, dtype=jnp.int32))
    return (blocks.reshape(MARKERS, PROBES), r_factor)
```

```python
import functools

import jax
import jax.numpy as jnp
from jax import lax
from jax.experimental import pallas as pl
from jax.experimental.pallas import tpu as pltpu
from jax.sharding import PartitionSpec as P

pinned = pltpu.with_memory_space_constraint
MESH = pl.DeviceIdType.MESH
F32 = jnp.float32
BF16 = jnp.bfloat16
NT = (((1,), (1,)), ((), ()))
PROBES = 64
CHUNKS = 8
VMEM_LIMIT = 48 * 2**20
DEPTH = 4
PANEL = 8
OFFSETS = {8: (4, 3, 5, 2, 6, 1, 7, 0), 4: (2, 1, 3, 0), 2: (1, 0)}
SCHEDULE = (
    "meet", "gram", "project0", "project1", "gramC", "project2", "near0", "project3", "near1",
    "near2", "near3", "plane0", "gramXY", "plane1", "plane2", "plane3", "axis0", "axis1",
    "gramZ", "axis2", "axis3", "gramAll", "factor", "finish",
)


def split3(value):
    high = value.astype(BF16)
    rest = value - high.astype(F32)
    middle = rest.astype(BF16)
    low = (rest - middle.astype(F32)).astype(BF16)
    return high, middle, low


def factor_panel(below, base):
    size = below.shape[0]
    cols = [jnp.broadcast_to(below[:, base + q : base + q + 1], (size, 128)) for q in range(PANEL)]
    rows = [below[q : q + 1] for q in range(PANEL)]
    for q in range(PANEL):
        pivot = cols[q][q : q + 1]
        scale = lax.rsqrt(pivot)
        scale = scale * (1.5 - 0.5 * pivot * scale * scale)
        cols[q] = cols[q] * scale
        rows[q] = rows[q] * scale
        for later in range(q + 1, PANEL):
            factor = cols[q][later : later + 1]
            cols[later] = cols[later] - cols[q] * factor
            rows[later] = rows[later] - rows[q] * factor
    rest = None
    if size > PANEL:
        rest = below[PANEL:]
        for q in range(PANEL):
            rest = rest - cols[q][PANEL:] * rows[q]
    return jnp.concatenate(rows, axis=0), rest


def finish_kernel(sum_ref, work_ref, projected_ref, r_ref):
    full = work_ref[...]
    row = lax.broadcasted_iota(jnp.int32, full.shape, 0)
    lane = lax.broadcasted_iota(jnp.int32, full.shape, 1)
    r_ref[...] = jnp.where(lane >= row, full, 0.0)[:, :PROBES]
    high = jnp.where(lane >= PROBES, full, 0.0)
    low = pltpu.roll(high, PROBES, 1)
    for half, inverse in enumerate((low, high)):
        projected_ref[pl.ds(16 * half, 16)] = lax.dot_general(
            sum_ref[...], inverse, NT, precision=lax.Precision.HIGHEST, preferred_element_type=F32
        )


def kernel(sizes, schedule, g_hbm, p_hbm, sum_ref, work_ref, g_buf, p_buf, split, ya, yb, ca, cb,
           ra1, rb1, sa1, sb1, ra2, rb2, total2, rz, gram_own, gram_c, gram_xy, gram_z, gram_all, work,
           load_sem, core_send, core_recv, one_send, one_recv, two_send, two_recv,
           z_send, z_recv, gram_send, gram_recv):
    nz, ny, nx = sizes
    groups = nz // 2
    offsets = OFFSETS[nz]
    me = lax.axis_index("rows")
    core = lax.rem(me, 2)
    x = lax.rem(me // 2, nx)
    y = lax.rem(me // (2 * nx), ny)
    z = me // (2 * nx * ny)

    def device(z=z, y=y, x=x, core=core):
        return (((z * ny + y) * nx + x) * 2 + core,)

    def ahead(position, offset, size):
        return lax.rem(position + offset, size)

    barrier = pltpu.get_barrier_semaphore()
    peers = [device(core=1 - core)]
    others = [(dy, dx) for dy in range(ny) for dx in range(nx) if dy or dx]
    others.sort(key=lambda d: -min(d[0], ny - d[0]) - min(d[1], nx - d[1]))
    peers += [device(y=ahead(y, dy, ny), x=ahead(x, dx, nx)) for dy, dx in others]
    peers += [device(z=ahead(z, o, nz)) for o in range(1, nz)]
    for peer in peers:
        pl.semaphore_signal(barrier, inc=1, device_id=peer, device_id_type=MESH)

    columns = g_hbm.shape[1] // CHUNKS

    def part(j):
        return (slice(None), pl.ds(j * columns, columns))

    loads = [
        [pltpu.make_async_copy(p_hbm.at[part(j)], p_buf.at[part(j)], load_sem.at[0, j]),
         pltpu.make_async_copy(g_hbm.at[part(j)], g_buf.at[part(j)], load_sem.at[1, j])]
        for j in range(CHUNKS)
    ]
    for pair in loads[:DEPTH]:
        for load in pair:
            load.start()
    sketch = jnp.zeros((PROBES, g_hbm.shape[0]), F32)
    for j in range(CHUNKS):
        for load in loads[j]:
            load.wait()
        if j + DEPTH < CHUNKS:
            for load in loads[j + DEPTH]:
                load.start()
        sketch += lax.dot_general(p_buf[part(j)], g_buf[part(j)], NT, preferred_element_type=F32)
    pieces = split3(sketch)
    for i, piece in enumerate(pieces):
        split[pl.ds(i * PROBES, PROBES)] = piece

    sent = []

    def copy(src, dst, send_sem, recv_sem, to):
        done = pltpu.make_async_remote_copy(
            src_ref=src, dst_ref=dst, send_sem=send_sem, recv_sem=recv_sem,
            device_id=to, device_id_type=MESH,
        )
        done.start()
        sent.append(done)
        return done

    left = lax.broadcasted_iota(jnp.int32, (16, 128), 1) < PROBES
    pending = {}

    def spread(buffer, mine, targets, sem0):
        return [
            copy(buffer.at[mine], buffer.at[mine], gram_send.at[sem0 + i], gram_recv.at[sem0 + i], to)
            for i, to in enumerate(targets)
        ]

    def total(arrived):
        for done in pending["gram"]:
            done.wait_recv()
        value = arrived[0]
        for i in range(1, arrived.shape[0]):
            value = value + arrived[i]
        return value

    def meet():
        pl.semaphore_wait(barrier, len(peers))

    def gram():
        full = split[...]
        product = sum(
            lax.dot_general(full, piece, NT, preferred_element_type=F32) for piece in pieces[::-1]
        )
        product = product[2 * PROBES :] + product[PROBES : 2 * PROBES] + product[:PROBES]
        packed = jnp.concatenate([product[:32], product[32:]], axis=1)
        gram_own[...] = packed.reshape(2, 16, 128)
        gram_c[core] = gram_own[core]
        pending["gram"] = [
            copy(gram_own.at[1 - core], gram_c.at[core], gram_send.at[0], gram_recv.at[0],
                 device(core=1 - core))
        ]

    def gram_core():
        mine = y * nx + x
        gram_xy[mine] = total(gram_c)
        to = [device(y=ahead(y, dy, ny), x=ahead(x, dx, nx)) for dy, dx in others]
        pending["gram"] = spread(gram_xy, mine, to, 1)

    def gram_plane():
        gram_z[z] = total(gram_xy)
        far = sorted(range(1, nz), key=lambda o: -min(o, nz - o))
        to = [device(z=ahead(z, o, nz)) for o in far]
        pending["gram"] = spread(gram_z, z, to, nx * ny)

    def gram_axis():
        gram_all[core] = total(gram_z)
        pending["gram"] = spread(gram_all, core, [device(core=1 - core)], nx * ny + nz - 1)

    def gram_whole():
        for done in pending["gram"]:
            done.wait_recv()
        value = gram_all[...].reshape(32, 128)
        row = lax.broadcasted_iota(jnp.int32, (32, 128), 0)
        lane = lax.broadcasted_iota(jnp.int32, (32, 128), 1)
        upper = jnp.where(lane == row + PROBES, 1.0, 0.0)
        lower = jnp.where(lane == row + PROBES + 32, 1.0, 0.0)
        work[:32] = jnp.where(lane < PROBES, value, upper)
        work[32:] = jnp.where(lane < PROBES, pltpu.roll(value, PROBES, 1), lower)

    def factor():
        rest = work[...]
        for base in range(0, PROBES, PANEL):
            done, rest = factor_panel(rest, base)
            work_ref[pl.ds(base, PANEL)] = done

    def project(g):
        for zz in range(2):
            z_to = ahead(z, offsets[2 * g + zz], nz)
            for y_to in range(ny):
                start = pl.multiple_of((z_to * ny + y_to) * 256, 256)
                out = jnp.dot(split[...], g_buf[:, pl.ds(start, 256)], preferred_element_type=F32)
                out = out[2 * PROBES :] + out[PROBES : 2 * PROBES] + out[:PROBES]
                turned = jnp.concatenate([out[:, :128], out[:, 128:]], axis=0).T
                for x_low in range(2):
                    for c in range(2):
                        at = 64 * x_low + 32 * c
                        top, bottom = turned[at : at + 16], turned[at + 16 : at + 32]
                        low = jnp.where(left, top, pltpu.roll(bottom, PROBES, 1))
                        high = jnp.where(left, pltpu.roll(top, PROBES, 1), bottom)
                        for x_to, block in ((x_low, low), (x_low + 2, high)):
                            ya[c, g, x_to, 2 * y_to + zz] = block[:8]
                            yb[c, g, y_to, 2 * x_to + zz] = block[8:]
        to = device(core=1 - core)
        pending["core", g] = [
            copy(ya.at[1 - core, g], ca.at[g], core_send.at[g, 0], core_recv.at[g, 0], to),
            copy(yb.at[1 - core, g], cb.at[g], core_send.at[g, 1], core_recv.at[g, 1], to),
        ]

    def near(g):
        from_a, from_b = pending["core", g]
        from_a.wait_recv()
        ya[core, g] = ya[core, g] + ca[g]
        first = [
            copy(ya.at[core, g, ahead(x, o, nx)], ra1.at[g, o - 1],
                 one_send.at[g, 0, o - 1], one_recv.at[g, 0, o - 1], device(x=ahead(x, o, nx)))
            for o in range(1, nx)
        ]
        from_b.wait_recv()
        yb[core, g] = yb[core, g] + cb[g]
        second = [
            copy(yb.at[core, g, ahead(y, o, ny)], rb1.at[g, o - 1],
                 one_send.at[g, 1, o - 1], one_recv.at[g, 1, o - 1], device(y=ahead(y, o, ny)))
            for o in range(1, ny)
        ]
        pending["one", g] = first, second

    def plane(g):
        first, second = pending["one", g]
        for done in first:
            done.wait_recv()
        value = ya[core, g, x]
        for o in range(1, nx):
            value = value + ra1[g, o - 1]
        sa1[g] = value
        first = [
            copy(sa1.at[g, pl.ds(2 * ahead(y, o, ny), 2)], ra2.at[g, o - 1],
                 two_send.at[g, 0, o - 1], two_recv.at[g, 0, o - 1], device(y=ahead(y, o, ny)))
            for o in range(1, ny)
        ]
        for done in second:
            done.wait_recv()
        value = yb[core, g, y]
        for o in range(1, ny):
            value = value + rb1[g, o - 1]
        sb1[g] = value
        second = [
            copy(sb1.at[g, pl.ds(2 * ahead(x, o, nx), 2)], rb2.at[g, o - 1],
                 two_send.at[g, 1, o - 1], two_recv.at[g, 1, o - 1], device(x=ahead(x, o, nx)))
            for o in range(1, nx)
        ]
        pending["two", g] = first, second

    pending["z"] = []

    def axis(g):
        first, second = pending["two", g]
        for done in first + second:
            done.wait_recv()
        value_a = sa1[g, pl.ds(2 * y, 2)]
        for o in range(1, ny):
            value_a = value_a + ra2[g, o - 1]
        value_b = sb1[g, pl.ds(2 * x, 2)]
        for o in range(1, nx):
            value_b = value_b + rb2[g, o - 1]
        for zz in range(2):
            slot = 2 * g + zz
            total2[slot, 0] = value_a[zz]
            total2[slot, 1] = value_b[zz]
            if offsets[slot]:
                pending["z"].append(
                    copy(total2.at[slot], rz.at[slot], z_send.at[slot], z_recv.at[slot],
                         device(z=ahead(z, offsets[slot], nz)))
                )

    def finish():
        for done in pending["z"]:
            done.wait_recv()
        value = total2[nz - 1]
        for slot in range(nz - 1):
            value = value + rz[slot]
        sum_ref[...] = value.reshape(16, 128)

    steps = {
        "meet": meet, "gram": gram, "gramC": gram_core, "gramXY": gram_plane, "gramZ": gram_axis,
        "gramAll": gram_whole, "factor": factor, "finish": finish,
    }
    for g in range(groups):
        steps[f"project{g}"] = functools.partial(project, g)
        steps[f"near{g}"] = functools.partial(near, g)
        steps[f"plane{g}"] = functools.partial(plane, g)
        steps[f"axis{g}"] = functools.partial(axis, g)
    for step in schedule:
        if step in steps:
            steps[step]()
    for done in sent:
        done.wait_send()


def build(mesh, sizes, schedule=SCHEDULE):
    nz, ny, nx = sizes
    groups = nz // 2

    def step(genotypes, probes):
        samples, markers = genotypes.shape
        vmem = pltpu.VMEM
        scratch = [
            vmem((samples, markers), BF16),
            vmem((PROBES, markers), BF16),
            vmem((3 * PROBES, samples), BF16),
            vmem((2, groups, nx, 2 * ny, 8, 128), F32),
            vmem((2, groups, ny, 2 * nx, 8, 128), F32),
            vmem((groups, nx, 2 * ny, 8, 128), F32),
            vmem((groups, ny, 2 * nx, 8, 128), F32),
            vmem((groups, max(nx - 1, 1), 2 * ny, 8, 128), F32),
            vmem((groups, max(ny - 1, 1), 2 * nx, 8, 128), F32),
            vmem((groups, 2 * ny, 8, 128), F32),
            vmem((groups, 2 * nx, 8, 128), F32),
            vmem((groups, max(ny - 1, 1), 2, 8, 128), F32),
            vmem((groups, max(nx - 1, 1), 2, 8, 128), F32),
            vmem((nz, 2, 8, 128), F32),
            vmem((nz - 1, 2, 8, 128), F32),
            vmem((2, 16, 128), F32),
            vmem((2, 16, 128), F32),
            vmem((ny * nx, 16, 128), F32),
            vmem((nz, 16, 128), F32),
            vmem((2, 16, 128), F32),
            vmem((PROBES, 128), F32),
            pltpu.SemaphoreType.DMA((2, CHUNKS)),
        ]
        most = max(nx, ny) - 1
        for shape in ((groups, 2), (groups, 2, most), (groups, 2, most), (nz,), (nx * ny + nz,)):
            scratch += [pltpu.SemaphoreType.DMA(shape)] * 2
        whole = pl.BlockSpec(memory_space=pltpu.VMEM)
        summed, factors = pl.pallas_call(
            functools.partial(kernel, sizes, schedule),
            out_shape=(
                jax.ShapeDtypeStruct((16, 128), F32),
                jax.ShapeDtypeStruct((PROBES, 128), F32),
            ),
            in_specs=[pl.BlockSpec(memory_space=pltpu.HBM)] * 2,
            out_specs=(whole, whole),
            scratch_shapes=scratch,
            compiler_params=pltpu.CompilerParams(
                collective_id=0, has_side_effects=True, vmem_limit_bytes=VMEM_LIMIT
            ),
            name="range_finder",
        )(pinned(genotypes, pltpu.HBM), pinned(probes.T, pltpu.HBM))
        return pl.pallas_call(
            finish_kernel,
            out_shape=(
                jax.ShapeDtypeStruct((32, PROBES), F32),
                jax.ShapeDtypeStruct((PROBES, PROBES), F32),
            ),
            in_specs=[whole, whole],
            out_specs=(whole, whole),
            compiler_params=pltpu.CompilerParams(vmem_limit_bytes=4 * 2**20),
            name="finish",
        )(summed, factors)

    return jax.shard_map(
        step,
        mesh=mesh,
        in_specs=(P("rows", None), P()),
        out_specs=(P("rows", None), P()),
        check_vma=False,
    )


def solution(mesh):
    return build(mesh, (8, 4, 4))
```

```python
import functools

import jax
import jax.numpy as jnp
from jax import lax
from jax.experimental import pallas as pl
from jax.experimental.pallas import tpu as pltpu
from jax.sharding import PartitionSpec as P

pinned = pltpu.with_memory_space_constraint
MESH = pl.DeviceIdType.MESH
F32 = jnp.float32
BF16 = jnp.bfloat16
NT = (((1,), (1,)), ((), ()))
PROBES = 64
CHUNKS = 8
VMEM_LIMIT = 48 * 2**20
DEPTH = 5
PANEL = 8
OFFSETS = {8: (4, 3, 5, 2, 6, 1, 7, 0), 4: (2, 1, 3, 0)}
NEAREST = {8: (0, 0), 4: (1, 3)}
BATCHES = {8: ((0, 2), (2, 4), (4, 6), (6, 8)), 4: ((0, 1), (1, 3), (3, 4))}
UNITS = {8: ((0, 2), (2, 4), (4, 6), (6, 8)), 4: ((0, 1), (3, 4))}
SCHEDULES = {
    8: ("meet", "gram", "project0", "gramC", "project1", "near0", "project2", "near1", "project3", "near2", "near3", "plane0", "gramXY", "plane1", "plane2", "axis0", "plane3", "axis1", "gramZ", "axis2", "axis3", "gramAll", "factor", "finish",
    ),
    4: (
        "meet", "gram", "project0", "project1", "project2", "gramC", "near0", "along", "gramXY",
        "near1", "plane0", "plane1", "axis0", "axis1", "gramZ", "gramAll", "factor", "finish",
    ),
}


def split3(value):
    high = value.astype(BF16)
    rest = value - high.astype(F32)
    middle = rest.astype(BF16)
    low = (rest - middle.astype(F32)).astype(BF16)
    return high, middle, low


def factor_panel(below, base):
    size = below.shape[0]
    cols = [jnp.broadcast_to(below[:, base + q : base + q + 1], (size, 128)) for q in range(PANEL)]
    rows = [below[q : q + 1] for q in range(PANEL)]
    for q in range(PANEL):
        pivot = cols[q][q : q + 1]
        scale = lax.rsqrt(pivot)
        scale = scale * (1.5 - 0.5 * pivot * scale * scale)
        cols[q] = cols[q] * scale
        rows[q] = rows[q] * scale
        for later in range(q + 1, PANEL):
            factor = cols[q][later : later + 1]
            cols[later] = cols[later] - cols[q] * factor
            rows[later] = rows[later] - rows[q] * factor
    rest = None
    if size > PANEL:
        rest = below[PANEL:]
        for q in range(PANEL):
            rest = rest - cols[q][PANEL:] * rows[q]
    return jnp.concatenate(rows, axis=0), rest


def finish_kernel(sum_ref, work_ref, projected_ref, r_ref):
    full = work_ref[...]
    row = lax.broadcasted_iota(jnp.int32, full.shape, 0)
    lane = lax.broadcasted_iota(jnp.int32, full.shape, 1)
    r_ref[...] = jnp.where(lane >= row, full, 0.0)[:, :PROBES]
    high = jnp.where(lane >= PROBES, full, 0.0)
    low = pltpu.roll(high, PROBES, 1)
    for half, inverse in enumerate((low, high)):
        projected_ref[pl.ds(16 * half, 16)] = lax.dot_general(
            sum_ref[...], inverse, NT, precision=lax.Precision.HIGHEST, preferred_element_type=F32
        )


def kernel(sizes, schedule, g_hbm, p_hbm, sum_ref, work_ref, g_buf, p_buf, split, ya, yb, ca, cb,
           za, zb, ra1, rb1, sa1, sb1, ra2, rb2, total2, rz, gram_own, gram_c, gram_xy, gram_z, gram_all, work,
           load_sem, core_send, core_recv, along_send, along_recv, one_send, one_recv, two_send, two_recv,
           z_send, z_recv, gram_send, gram_recv):
    nz, ny, nx = sizes
    offsets = OFFSETS[nz]
    nearest = NEAREST[nz]
    batches = BATCHES[nz]
    units = UNITS[nz]
    me = lax.axis_index("rows")
    core = lax.rem(me, 2)
    x = lax.rem(me // 2, nx)
    y = lax.rem(me // (2 * nx), ny)
    z = me // (2 * nx * ny)

    def device(z=z, y=y, x=x, core=core):
        return (((z * ny + y) * nx + x) * 2 + core,)

    def ahead(position, offset, size):
        return lax.rem(position + offset, size)

    columns = g_hbm.shape[1] // CHUNKS

    def part(j):
        return (slice(None), pl.ds(j * columns, columns))

    loads = [
        [pltpu.make_async_copy(p_hbm.at[part(j)], p_buf.at[part(j)], load_sem.at[0, j]),
         pltpu.make_async_copy(g_hbm.at[part(j)], g_buf.at[part(j)], load_sem.at[1, j])]
        for j in range(CHUNKS)
    ]
    for pair in loads[:DEPTH]:
        for load in pair:
            load.start()
    barrier = pltpu.get_barrier_semaphore()
    peers = [device(core=1 - core)]
    others = [(dy, dx) for dy in range(ny) for dx in range(nx) if dy or dx]
    others.sort(key=lambda d: -min(d[0], ny - d[0]) - min(d[1], nx - d[1]))
    peers += [device(y=ahead(y, dy, ny), x=ahead(x, dx, nx)) for dy, dx in others]
    peers += [device(z=ahead(z, o, nz)) for o in range(1, nz)]
    for peer in peers:
        pl.semaphore_signal(barrier, inc=1, device_id=peer, device_id_type=MESH)

    sketch = jnp.zeros((PROBES, g_hbm.shape[0]), F32)
    for j in range(CHUNKS):
        for load in loads[j]:
            load.wait()
        if j + DEPTH < CHUNKS:
            for load in loads[j + DEPTH]:
                load.start()
        sketch += lax.dot_general(p_buf[part(j)], g_buf[part(j)], NT, preferred_element_type=F32)
    pieces = split3(sketch)
    for i, piece in enumerate(pieces):
        split[pl.ds(i * PROBES, PROBES)] = piece

    sent = []

    def copy(src, dst, send_sem, recv_sem, to):
        done = pltpu.make_async_remote_copy(
            src_ref=src, dst_ref=dst, send_sem=send_sem, recv_sem=recv_sem,
            device_id=to, device_id_type=MESH,
        )
        done.start()
        sent.append(done)
        return done

    left = lax.broadcasted_iota(jnp.int32, (16, 128), 1) < PROBES
    pending = {}

    def spread(buffer, mine, targets, sem0):
        return [
            copy(buffer.at[mine], buffer.at[mine], gram_send.at[sem0 + i], gram_recv.at[sem0 + i], to)
            for i, to in enumerate(targets)
        ]

    def total(arrived):
        for done in pending["gram"]:
            done.wait_recv()
        value = arrived[0]
        for i in range(1, arrived.shape[0]):
            value = value + arrived[i]
        return value

    def meet():
        pl.semaphore_wait(barrier, len(peers))

    def gram():
        full = split[...]
        product = sum(
            lax.dot_general(full, piece, NT, preferred_element_type=F32) for piece in pieces[::-1]
        )
        product = product[2 * PROBES :] + product[PROBES : 2 * PROBES] + product[:PROBES]
        packed = jnp.concatenate([product[:32], product[32:]], axis=1)
        gram_own[...] = packed.reshape(2, 16, 128)
        gram_c[core] = gram_own[core]
        pending["gram"] = [
            copy(gram_own.at[1 - core], gram_c.at[core], gram_send.at[0], gram_recv.at[0],
                 device(core=1 - core))
        ]

    def gram_core():
        mine = y * nx + x
        gram_xy[mine] = total(gram_c)
        to = [device(y=ahead(y, dy, ny), x=ahead(x, dx, nx)) for dy, dx in others]
        pending["gram"] = spread(gram_xy, mine, to, 1)

    def gram_plane():
        gram_z[z] = total(gram_xy)
        far = sorted(range(1, nz), key=lambda o: -min(o, nz - o))
        to = [device(z=ahead(z, o, nz)) for o in far]
        pending["gram"] = spread(gram_z, z, to, nx * ny)

    def gram_axis():
        gram_all[core] = total(gram_z)
        pending["gram"] = spread(gram_all, core, [device(core=1 - core)], nx * ny + nz - 1)

    def gram_whole():
        for done in pending["gram"]:
            done.wait_recv()
        value = gram_all[...].reshape(32, 128)
        row = lax.broadcasted_iota(jnp.int32, (32, 128), 0)
        lane = lax.broadcasted_iota(jnp.int32, (32, 128), 1)
        upper = jnp.where(lane == row + PROBES, 1.0, 0.0)
        lower = jnp.where(lane == row + PROBES + 32, 1.0, 0.0)
        work[:32] = jnp.where(lane < PROBES, value, upper)
        work[32:] = jnp.where(lane < PROBES, pltpu.roll(value, PROBES, 1), lower)

    def factor():
        rest = work[...]
        for base in range(0, PROBES, PANEL):
            done, rest = factor_panel(rest, base)
            work_ref[pl.ds(base, PANEL)] = done

    def project(i):
        first, last = batches[i]
        for slot in range(first, last):
            z_to = ahead(z, offsets[slot], nz)
            for y_to in range(ny):
                start = pl.multiple_of((z_to * ny + y_to) * 256, 256)
                out = jnp.dot(split[...], g_buf[:, pl.ds(start, 256)], preferred_element_type=F32)
                out = out[2 * PROBES :] + out[PROBES : 2 * PROBES] + out[:PROBES]
                turned = jnp.concatenate([out[:, :128], out[:, 128:]], axis=0).T
                for x_low in range(2):
                    for c in range(2):
                        at = 64 * x_low + 32 * c
                        top, bottom = turned[at : at + 16], turned[at + 16 : at + 32]
                        low = jnp.where(left, top, pltpu.roll(bottom, PROBES, 1))
                        high = jnp.where(left, pltpu.roll(top, PROBES, 1), bottom)
                        for x_to, block in ((x_low, low), (x_low + 2, high)):
                            ya[c, slot, x_to, y_to] = block[:8]
                            yb[c, slot, y_to, x_to] = block[8:]
        to = device(core=1 - core)
        slots = pl.ds(first, last - first)
        pending["core", i] = [
            copy(ya.at[1 - core, slots], ca.at[slots], core_send.at[i, 0], core_recv.at[i, 0], to),
            copy(yb.at[1 - core, slots], cb.at[slots], core_send.at[i, 1], core_recv.at[i, 1], to),
        ]

    def chip_sum(which, slots):
        mine, other = ((ya, ca), (yb, cb))[which]
        for i, (first, last) in enumerate(batches):
            if first < slots[1] and slots[0] < last and (i, which) not in settled:
                settled.add((i, which))
                pending["core", i][which].wait_recv()
        at = pl.ds(slots[0], slots[1] - slots[0])
        mine[core, at] = mine[core, at] + other[at]

    settled = set()

    def along():
        out = []
        for which, (mine, landing) in enumerate(((ya, za), (yb, zb))):
            chip_sum(which, nearest)
            for i, slot in enumerate(range(*nearest)):
                out.append(
                    copy(mine.at[core, slot], landing.at[i], along_send.at[which, i],
                         along_recv.at[which, i], device(z=ahead(z, offsets[slot], nz)))
                )
        pending["along"] = out

    def near(i):
        first, last = units[i]
        slots = pl.ds(first, last - first)
        out = []
        for which, (mine, landing, size, here) in enumerate(((ya, ra1, nx, x), (yb, rb1, ny, y))):
            chip_sum(which, units[i])
            if last == nz and "along" in pending:
                for done in pending["along"][2 * which : 2 * which + 2]:
                    done.wait_recv()
                arrived = (za, zb)[which]
                mine[core, nz - 1] = mine[core, nz - 1] + (arrived[0] + arrived[1])
            for o in (2, 1, 3) if size == 4 else range(1, size):
                to_there = ahead(here, o, size)
                to = device(x=to_there) if which == 0 else device(y=to_there)
                out.append(
                    copy(mine.at[core, slots, to_there], landing.at[slots, o - 1],
                         one_send.at[i, which, o - 1], one_recv.at[i, which, o - 1], to)
                )
        pending["one", i] = out

    def plane(i):
        first, last = units[i]
        slots = pl.ds(first, last - first)
        arriving = pending["one", i]
        out = []
        for which, (mine, landed, kept, landing, size, here, size2, here2) in enumerate((
            (ya, ra1, sa1, ra2, nx, x, ny, y), (yb, rb1, sb1, rb2, ny, y, nx, x),
        )):
            for done in arriving[: size - 1]:
                done.wait_recv()
            arriving = arriving[size - 1 :]
            value = mine[core, slots, here]
            for o in range(1, size):
                value = value + landed[slots, o - 1]
            kept[slots] = value
            for o in (2, 1, 3) if size2 == 4 else range(1, size2):
                to_there = ahead(here2, o, size2)
                to = device(y=to_there) if which == 0 else device(x=to_there)
                out.append(
                    copy(kept.at[slots, to_there], landing.at[slots, o - 1],
                         two_send.at[i, which, o - 1], two_recv.at[i, which, o - 1], to)
                )
        pending["two", i] = out

    pending["z"] = []

    def axis(i):
        first, last = units[i]
        slots = pl.ds(first, last - first)
        for done in pending["two", i]:
            done.wait_recv()
        for which, (kept, landed, size, here) in enumerate(((sa1, ra2, ny, y), (sb1, rb2, nx, x))):
            value = kept[slots, here]
            for o in range(1, size):
                value = value + landed[slots, o - 1]
            total2[slots, which] = value
        for slot in range(first, last):
            if offsets[slot]:
                pending["z"].append(
                    (slot, copy(total2.at[slot], rz.at[slot], z_send.at[slot], z_recv.at[slot],
                                device(z=ahead(z, offsets[slot], nz))))
                )

    def finish():
        value = total2[nz - 1]
        for slot, done in pending["z"]:
            done.wait_recv()
            value = value + rz[slot]
        sum_ref[...] = value.reshape(16, 128)

    steps = {
        "meet": meet, "gram": gram, "gramC": gram_core, "gramXY": gram_plane, "gramZ": gram_axis,
        "gramAll": gram_whole, "factor": factor, "finish": finish,
    }
    steps["along"] = along
    for i in range(len(batches)):
        steps[f"project{i}"] = functools.partial(project, i)
    for i in range(len(units)):
        steps[f"near{i}"] = functools.partial(near, i)
        steps[f"plane{i}"] = functools.partial(plane, i)
        steps[f"axis{i}"] = functools.partial(axis, i)
    for step in schedule:
        if step in steps:
            steps[step]()
    for done in sent:
        done.wait_send()


def build(mesh, sizes):
    nz, ny, nx = sizes
    schedule = SCHEDULES[nz]

    def step(genotypes, probes):
        samples, markers = genotypes.shape
        vmem = pltpu.VMEM
        scratch = [
            vmem((samples, markers), BF16),
            vmem((PROBES, markers), BF16),
            vmem((3 * PROBES, samples), BF16),
            vmem((2, nz, nx, ny, 8, 128), F32),
            vmem((2, nz, ny, nx, 8, 128), F32),
            vmem((nz, nx, ny, 8, 128), F32),
            vmem((nz, ny, nx, 8, 128), F32),
            vmem((2, nx, ny, 8, 128), F32),
            vmem((2, ny, nx, 8, 128), F32),
            vmem((nz, max(nx - 1, 1), ny, 8, 128), F32),
            vmem((nz, max(ny - 1, 1), nx, 8, 128), F32),
            vmem((nz, ny, 8, 128), F32),
            vmem((nz, nx, 8, 128), F32),
            vmem((nz, max(ny - 1, 1), 8, 128), F32),
            vmem((nz, max(nx - 1, 1), 8, 128), F32),
            vmem((nz, 2, 8, 128), F32),
            vmem((nz, 2, 8, 128), F32),
            vmem((2, 16, 128), F32),
            vmem((2, 16, 128), F32),
            vmem((ny * nx, 16, 128), F32),
            vmem((nz, 16, 128), F32),
            vmem((2, 16, 128), F32),
            vmem((PROBES, 128), F32),
            pltpu.SemaphoreType.DMA((2, CHUNKS)),
        ]
        most = max(nx, ny) - 1
        units = len(UNITS[nz])
        for shape in ((len(BATCHES[nz]), 2), (2, 2), (units, 2, most), (units, 2, most), (nz,),
                      (nx * ny + nz,)):
            scratch += [pltpu.SemaphoreType.DMA(shape)] * 2
        whole = pl.BlockSpec(memory_space=pltpu.VMEM)
        summed, factors = pl.pallas_call(
            functools.partial(kernel, sizes, schedule),
            out_shape=(
                jax.ShapeDtypeStruct((16, 128), F32),
                jax.ShapeDtypeStruct((PROBES, 128), F32),
            ),
            in_specs=[pl.BlockSpec(memory_space=pltpu.HBM)] * 2,
            out_specs=(whole, whole),
            scratch_shapes=scratch,
            compiler_params=pltpu.CompilerParams(
                collective_id=0, has_side_effects=True, vmem_limit_bytes=VMEM_LIMIT
            ),
            name="range_finder",
        )(pinned(genotypes, pltpu.HBM), pinned(probes.T, pltpu.HBM))
        return pl.pallas_call(
            finish_kernel,
            out_shape=(
                jax.ShapeDtypeStruct((32, PROBES), F32),
                jax.ShapeDtypeStruct((PROBES, PROBES), F32),
            ),
            in_specs=[whole, whole],
            out_specs=(whole, whole),
            compiler_params=pltpu.CompilerParams(vmem_limit_bytes=4 * 2**20),
            name="finish",
        )(summed, factors)

    return jax.shard_map(
        step,
        mesh=mesh,
        in_specs=(P("rows", None), P()),
        out_specs=(P("rows", None), P()),
        check_vma=False,
    )


def solution(mesh):
    return build(mesh, (8, 4, 4))
```

```python
import functools

import jax
import jax.numpy as jnp
from jax import lax
from jax.experimental import pallas as pl
from jax.experimental.pallas import tpu as pltpu
from jax.sharding import PartitionSpec as P

pinned = pltpu.with_memory_space_constraint
MESH = pl.DeviceIdType.MESH
F32 = jnp.float32
BF16 = jnp.bfloat16
NT = (((1,), (1,)), ((), ()))
PROBES = 64
CHUNKS = 8
VMEM_LIMIT = 48 * 2**20
DEPTH = 5
PANEL = 8
OFFSETS = {8: (4, 3, 5, 2, 6, 1, 7, 0), 4: (2, 1, 3, 0)}
NEAREST = {8: (0, 0), 4: (1, 3)}
BATCHES = {8: ((0, 2), (2, 4), (4, 6), (6, 8)), 4: ((0, 1), (1, 3), (3, 4))}
UNITS = {8: ((0, 2), (2, 4), (4, 6), (6, 8)), 4: ((0, 1), (3, 4))}
SCHEDULES = {
    8: ("meet", "gram", "project0", "gramC", "project1", "near0", "project2", "near1", "project3", "near2", "near3", "plane0", "gramXY", "plane1", "plane2", "axis0", "plane3", "axis1", "gramZ", "axis2", "axis3", "gramAll", "factor", "finish",
    ),
    4: (
        "meet", "gram", "project0", "project1", "project2", "gramC", "near0", "along", "gramXY",
        "near1", "plane0", "plane1", "axis0", "axis1", "gramZ", "gramAll", "factor", "finish",
    ),
}


def split3(value):
    high = value.astype(BF16)
    rest = value - high.astype(F32)
    middle = rest.astype(BF16)
    low = (rest - middle.astype(F32)).astype(BF16)
    return high, middle, low


def factor_panel(below, base):
    size = below.shape[0]
    cols = [jnp.broadcast_to(below[:, base + q : base + q + 1], (size, 128)) for q in range(PANEL)]
    rows = [below[q : q + 1] for q in range(PANEL)]
    for q in range(PANEL):
        pivot = cols[q][q : q + 1]
        scale = lax.rsqrt(pivot)
        scale = scale * (1.5 - 0.5 * pivot * scale * scale)
        cols[q] = cols[q] * scale
        rows[q] = rows[q] * scale
        for later in range(q + 1, PANEL):
            factor = cols[q][later : later + 1]
            cols[later] = cols[later] - cols[q] * factor
            rows[later] = rows[later] - rows[q] * factor
    rest = None
    if size > PANEL:
        rest = below[PANEL:]
        for q in range(PANEL):
            rest = rest - cols[q][PANEL:] * rows[q]
    return jnp.concatenate(rows, axis=0), rest


def finish_kernel(sum_ref, work_ref, projected_ref, r_ref):
    full = work_ref[...]
    row = lax.broadcasted_iota(jnp.int32, full.shape, 0)
    lane = lax.broadcasted_iota(jnp.int32, full.shape, 1)
    r_ref[...] = jnp.where(lane >= row, full, 0.0)[:, :PROBES]
    high = jnp.where(lane >= PROBES, full, 0.0)
    low = pltpu.roll(high, PROBES, 1)
    for half, inverse in enumerate((low, high)):
        projected_ref[pl.ds(16 * half, 16)] = lax.dot_general(
            sum_ref[...], inverse, NT, precision=lax.Precision.HIGHEST, preferred_element_type=F32
        )


def kernel(sizes, schedule, g_hbm, p_hbm, sum_ref, work_ref, g_buf, p_buf, sketch_ref, split, ya, yb, ca, cb,
           za, zb, ra1, rb1, sa1, sb1, ra2, rb2, total2, rz, gram_own, gram_c, gram_xy, gram_z, gram_all, work,
           load_sem, core_send, core_recv, along_send, along_recv, one_send, one_recv, two_send, two_recv,
           z_send, z_recv, gram_send, gram_recv):
    nz, ny, nx = sizes
    offsets = OFFSETS[nz]
    nearest = NEAREST[nz]
    batches = BATCHES[nz]
    units = UNITS[nz]
    me = lax.axis_index("rows")
    core = lax.rem(me, 2)
    x = lax.rem(me // 2, nx)
    y = lax.rem(me // (2 * nx), ny)
    z = me // (2 * nx * ny)

    def device(z=z, y=y, x=x, core=core):
        return (((z * ny + y) * nx + x) * 2 + core,)

    def ahead(position, offset, size):
        return lax.rem(position + offset, size)

    columns = g_hbm.shape[1] // CHUNKS

    def part(j):
        return (slice(None), pl.ds(j * columns, columns))

    loads = [
        [pltpu.make_async_copy(p_hbm.at[part(j)], p_buf.at[part(j)], load_sem.at[0, j]),
         pltpu.make_async_copy(g_hbm.at[part(j)], g_buf.at[part(j)], load_sem.at[1, j])]
        for j in range(CHUNKS)
    ]
    for pair in loads[:DEPTH]:
        for load in pair:
            load.start()
    barrier = pltpu.get_barrier_semaphore()
    peers = [device(core=1 - core)]
    others = [(dy, dx) for dy in range(ny) for dx in range(nx) if dy or dx]
    others.sort(key=lambda d: -min(d[0], ny - d[0]) - min(d[1], nx - d[1]))
    peers += [device(y=ahead(y, dy, ny), x=ahead(x, dx, nx)) for dy, dx in others]
    peers += [device(z=ahead(z, o, nz)) for o in range(1, nz)]
    for peer in peers:
        pl.semaphore_signal(barrier, inc=1, device_id=peer, device_id_type=MESH)

    for j in range(CHUNKS):
        for load in loads[j]:
            load.wait()
        if j + DEPTH < CHUNKS:
            for load in loads[j + DEPTH]:
                load.start()
        term = lax.dot_general(p_buf[part(j)], g_buf[part(j)], NT, preferred_element_type=F32)
        sketch_ref[...] = sketch_ref[...] + term if j else term
    pieces = split3(sketch_ref[...])
    for i, piece in enumerate(pieces):
        split[pl.ds(i * PROBES, PROBES)] = piece

    sent = []

    def copy(src, dst, send_sem, recv_sem, to):
        done = pltpu.make_async_remote_copy(
            src_ref=src, dst_ref=dst, send_sem=send_sem, recv_sem=recv_sem,
            device_id=to, device_id_type=MESH,
        )
        done.start()
        sent.append(done)
        return done

    left = lax.broadcasted_iota(jnp.int32, (16, 128), 1) < PROBES
    pending = {}

    def spread(buffer, mine, targets, sem0):
        return [
            copy(buffer.at[mine], buffer.at[mine], gram_send.at[sem0 + i], gram_recv.at[sem0 + i], to)
            for i, to in enumerate(targets)
        ]

    def total(arrived):
        for done in pending["gram"]:
            done.wait_recv()
        value = arrived[0]
        for i in range(1, arrived.shape[0]):
            value = value + arrived[i]
        return value

    def meet():
        pl.semaphore_wait(barrier, len(peers))

    def gram():
        full = split[...]
        product = sum(
            lax.dot_general(full, piece, NT, preferred_element_type=F32) for piece in pieces[::-1]
        )
        product = product[2 * PROBES :] + product[PROBES : 2 * PROBES] + product[:PROBES]
        packed = jnp.concatenate([product[:32], product[32:]], axis=1)
        gram_own[...] = packed.reshape(2, 16, 128)
        gram_c[core] = gram_own[core]
        pending["gram"] = [
            copy(gram_own.at[1 - core], gram_c.at[core], gram_send.at[0], gram_recv.at[0],
                 device(core=1 - core))
        ]

    def gram_core():
        mine = y * nx + x
        gram_xy[mine] = total(gram_c)
        to = [device(y=ahead(y, dy, ny), x=ahead(x, dx, nx)) for dy, dx in others]
        pending["gram"] = spread(gram_xy, mine, to, 1)

    def gram_plane():
        gram_z[z] = total(gram_xy)
        far = sorted(range(1, nz), key=lambda o: -min(o, nz - o))
        to = [device(z=ahead(z, o, nz)) for o in far]
        pending["gram"] = spread(gram_z, z, to, nx * ny)

    def gram_axis():
        gram_all[core] = total(gram_z)
        pending["gram"] = spread(gram_all, core, [device(core=1 - core)], nx * ny + nz - 1)

    def gram_whole():
        for done in pending["gram"]:
            done.wait_recv()
        value = gram_all[...].reshape(32, 128)
        row = lax.broadcasted_iota(jnp.int32, (32, 128), 0)
        lane = lax.broadcasted_iota(jnp.int32, (32, 128), 1)
        upper = jnp.where(lane == row + PROBES, 1.0, 0.0)
        lower = jnp.where(lane == row + PROBES + 32, 1.0, 0.0)
        work[:32] = jnp.where(lane < PROBES, value, upper)
        work[32:] = jnp.where(lane < PROBES, pltpu.roll(value, PROBES, 1), lower)

    def factor():
        rest = work[...]
        for base in range(0, PROBES, PANEL):
            done, rest = factor_panel(rest, base)
            work_ref[pl.ds(base, PANEL)] = done

    def project(i):
        first, last = batches[i]
        for slot in range(first, last):
            z_to = ahead(z, offsets[slot], nz)
            for y_to in range(ny):
                start = pl.multiple_of((z_to * ny + y_to) * 256, 256)
                out = jnp.dot(split[...], g_buf[:, pl.ds(start, 256)], preferred_element_type=F32)
                out = out[2 * PROBES :] + out[PROBES : 2 * PROBES] + out[:PROBES]
                turned = jnp.concatenate([out[:, :128], out[:, 128:]], axis=0).T
                for x_low in range(2):
                    for c in range(2):
                        at = 64 * x_low + 32 * c
                        top, bottom = turned[at : at + 16], turned[at + 16 : at + 32]
                        low = jnp.where(left, top, pltpu.roll(bottom, PROBES, 1))
                        high = jnp.where(left, pltpu.roll(top, PROBES, 1), bottom)
                        for x_to, block in ((x_low, low), (x_low + 2, high)):
                            ya[c, slot, x_to, y_to] = block[:8]
                            yb[c, slot, y_to, x_to] = block[8:]
        to = device(core=1 - core)
        slots = pl.ds(first, last - first)
        pending["core", i] = [
            copy(ya.at[1 - core, slots], ca.at[slots], core_send.at[i, 0], core_recv.at[i, 0], to),
            copy(yb.at[1 - core, slots], cb.at[slots], core_send.at[i, 1], core_recv.at[i, 1], to),
        ]

    def chip_sum(which, slots):
        mine, other = ((ya, ca), (yb, cb))[which]
        for i, (first, last) in enumerate(batches):
            if first < slots[1] and slots[0] < last and (i, which) not in settled:
                settled.add((i, which))
                pending["core", i][which].wait_recv()
        at = pl.ds(slots[0], slots[1] - slots[0])
        mine[core, at] = mine[core, at] + other[at]

    settled = set()

    def along():
        out = []
        for which, (mine, landing) in enumerate(((ya, za), (yb, zb))):
            chip_sum(which, nearest)
            for i, slot in enumerate(range(*nearest)):
                out.append(
                    copy(mine.at[core, slot], landing.at[i], along_send.at[which, i],
                         along_recv.at[which, i], device(z=ahead(z, offsets[slot], nz)))
                )
        pending["along"] = out

    def near(i):
        first, last = units[i]
        slots = pl.ds(first, last - first)
        out = []
        for which, (mine, landing, size, here) in enumerate(((ya, ra1, nx, x), (yb, rb1, ny, y))):
            chip_sum(which, units[i])
            if last == nz and "along" in pending:
                for done in pending["along"][2 * which : 2 * which + 2]:
                    done.wait_recv()
                arrived = (za, zb)[which]
                mine[core, nz - 1] = mine[core, nz - 1] + (arrived[0] + arrived[1])
            for o in (2, 1, 3) if size == 4 else range(1, size):
                to_there = ahead(here, o, size)
                to = device(x=to_there) if which == 0 else device(y=to_there)
                out.append(
                    copy(mine.at[core, slots, to_there], landing.at[slots, o - 1],
                         one_send.at[i, which, o - 1], one_recv.at[i, which, o - 1], to)
                )
        pending["one", i] = out

    def plane(i):
        first, last = units[i]
        slots = pl.ds(first, last - first)
        arriving = pending["one", i]
        out = []
        for which, (mine, landed, kept, landing, size, here, size2, here2) in enumerate((
            (ya, ra1, sa1, ra2, nx, x, ny, y), (yb, rb1, sb1, rb2, ny, y, nx, x),
        )):
            for done in arriving[: size - 1]:
                done.wait_recv()
            arriving = arriving[size - 1 :]
            value = mine[core, slots, here]
            for o in range(1, size):
                value = value + landed[slots, o - 1]
            kept[slots] = value
            for o in (2, 1, 3) if size2 == 4 else range(1, size2):
                to_there = ahead(here2, o, size2)
                to = device(y=to_there) if which == 0 else device(x=to_there)
                out.append(
                    copy(kept.at[slots, to_there], landing.at[slots, o - 1],
                         two_send.at[i, which, o - 1], two_recv.at[i, which, o - 1], to)
                )
        pending["two", i] = out

    pending["z"] = []

    def axis(i):
        first, last = units[i]
        slots = pl.ds(first, last - first)
        for done in pending["two", i]:
            done.wait_recv()
        for which, (kept, landed, size, here) in enumerate(((sa1, ra2, ny, y), (sb1, rb2, nx, x))):
            value = kept[slots, here]
            for o in range(1, size):
                value = value + landed[slots, o - 1]
            total2[slots, which] = value
        for slot in range(first, last):
            if offsets[slot]:
                pending["z"].append(
                    (slot, copy(total2.at[slot], rz.at[slot], z_send.at[slot], z_recv.at[slot],
                                device(z=ahead(z, offsets[slot], nz))))
                )

    def finish():
        value = total2[nz - 1]
        for slot, done in pending["z"]:
            done.wait_recv()
            value = value + rz[slot]
        sum_ref[...] = value.reshape(16, 128)

    steps = {
        "meet": meet, "gram": gram, "gramC": gram_core, "gramXY": gram_plane, "gramZ": gram_axis,
        "gramAll": gram_whole, "factor": factor, "finish": finish,
    }
    steps["along"] = along
    for i in range(len(batches)):
        steps[f"project{i}"] = functools.partial(project, i)
    for i in range(len(units)):
        steps[f"near{i}"] = functools.partial(near, i)
        steps[f"plane{i}"] = functools.partial(plane, i)
        steps[f"axis{i}"] = functools.partial(axis, i)
    for step in schedule:
        if step in steps:
            steps[step]()
    for done in sent:
        done.wait_send()


def build(mesh, sizes):
    nz, ny, nx = sizes
    schedule = SCHEDULES[nz]

    def step(genotypes, probes):
        samples, markers = genotypes.shape
        vmem = pltpu.VMEM
        scratch = [
            vmem((samples, markers), BF16),
            vmem((PROBES, markers), BF16),
            vmem((PROBES, samples), F32),
            vmem((3 * PROBES, samples), BF16),
            vmem((2, nz, nx, ny, 8, 128), F32),
            vmem((2, nz, ny, nx, 8, 128), F32),
            vmem((nz, nx, ny, 8, 128), F32),
            vmem((nz, ny, nx, 8, 128), F32),
            vmem((2, nx, ny, 8, 128), F32),
            vmem((2, ny, nx, 8, 128), F32),
            vmem((nz, max(nx - 1, 1), ny, 8, 128), F32),
            vmem((nz, max(ny - 1, 1), nx, 8, 128), F32),
            vmem((nz, ny, 8, 128), F32),
            vmem((nz, nx, 8, 128), F32),
            vmem((nz, max(ny - 1, 1), 8, 128), F32),
            vmem((nz, max(nx - 1, 1), 8, 128), F32),
            vmem((nz, 2, 8, 128), F32),
            vmem((nz, 2, 8, 128), F32),
            vmem((2, 16, 128), F32),
            vmem((2, 16, 128), F32),
            vmem((ny * nx, 16, 128), F32),
            vmem((nz, 16, 128), F32),
            vmem((2, 16, 128), F32),
            vmem((PROBES, 128), F32),
            pltpu.SemaphoreType.DMA((2, CHUNKS)),
        ]
        most = max(nx, ny) - 1
        units = len(UNITS[nz])
        for shape in ((len(BATCHES[nz]), 2), (2, 2), (units, 2, most), (units, 2, most), (nz,),
                      (nx * ny + nz,)):
            scratch += [pltpu.SemaphoreType.DMA(shape)] * 2
        whole = pl.BlockSpec(memory_space=pltpu.VMEM)
        summed, factors = pl.pallas_call(
            functools.partial(kernel, sizes, schedule),
            out_shape=(
                jax.ShapeDtypeStruct((16, 128), F32),
                jax.ShapeDtypeStruct((PROBES, 128), F32),
            ),
            in_specs=[pl.BlockSpec(memory_space=pltpu.HBM)] * 2,
            out_specs=(whole, whole),
            scratch_shapes=scratch,
            compiler_params=pltpu.CompilerParams(
                collective_id=0, has_side_effects=True, vmem_limit_bytes=VMEM_LIMIT
            ),
            name="range_finder",
        )(pinned(genotypes, pltpu.HBM), pinned(probes.T, pltpu.HBM))
        return pl.pallas_call(
            finish_kernel,
            out_shape=(
                jax.ShapeDtypeStruct((32, PROBES), F32),
                jax.ShapeDtypeStruct((PROBES, PROBES), F32),
            ),
            in_specs=[whole, whole],
            out_specs=(whole, whole),
            compiler_params=pltpu.CompilerParams(vmem_limit_bytes=4 * 2**20),
            name="finish",
        )(summed, factors)

    return jax.shard_map(
        step,
        mesh=mesh,
        in_specs=(P("rows", None), P()),
        out_specs=(P("rows", None), P()),
        check_vma=False,
    )


def solution(mesh):
    return build(mesh, (8, 4, 4))
```
